32 devices in a mesh: seq: 8 (over z, x), head: 4 (over y, core).
Axes of the slice: x: 2, y: 2, z: 4, core: 2. Of those that a mesh axis runs over, the one named last changes fastest.
Arguments:
- queries: bfloat16 [8192, 8192], P('seq', 'head'), may hold values from -6 to 6
- key_vectors: bfloat16 [8192, 8192], P('seq', 'head'), may hold values from -6 to 6
- value_vectors: bfloat16 [8192, 8192], P('seq', 'head'), may hold values from -6 to 6
- level_weight: float32 [8192, 1024], P('seq', 'head'), may hold values from 0.02 to 1
- gate_values: bfloat16 [8192, 8192], P(('seq', 'head')), may hold values from -6 to 6
- norm_gain: float32 [8192], replicated, may hold values from 0.5 to 1.5
Outputs:
- normed: bfloat16 [8192, 8192], P(('seq', 'head'))
The draws below stay inside these ranges and needn't reach their ends.
All inputs are finite; a program needn't handle non-finite values.
Results may differ from the reference program's by a relative error of at most 0.012.
Values may be sent and summed in bfloat16 or wider, within the bound.
No kernel may reach another device: no remote copies, remote signals or barrier semaphores. Data moves between devices by JAX's collectives and lax.ppermute only.
A program may use at most 128 MiB of HBM per device.

```python
import math
import jax
import jax.numpy as jnp
from jax import lax

HEADS = 64
HEAD_DIM = 128
TOK_DEV = 1024
LEVELS = 16
TOKENS = 8192
D = 8192
N_SEQ = 8


def level_of(stream_key, extent, pieces, smallest, top_value):
    def one(dim, parts):
        heights = jax.random.uniform(jax.random.fold_in(jax.random.fold_in(stream_key, 6), dim), (parts,), jnp.float32, smallest / len(pieces), top_value / len(pieces))
        return jnp.repeat(jnp.exp(heights), extent[dim] // parts).reshape((-1,) + (1,) * (len(extent) - dim - 1))

    factor_of = one(*pieces[0])
    for cut in pieces[1:]:
        factor_of = factor_of * one(*cut)
    return factor_of


def gaussian(rng, extent, deviation, limit, pieces=(), kind=jnp.bfloat16):
    entries = jax.random.normal(rng, extent, jnp.float32) * deviation
    if len(pieces) > 0:
        entries = level_of(rng, extent, pieces, -0.22, 0.18) * entries
    return jnp.clip(entries, min=-limit, max=limit).astype(kind)


def setup_inputs(seed: int = 0) -> dict:
    streams_of = jax.random.split(jax.random.key(seed), 7)
    return {
        "queries": gaussian(streams_of[0], (TOKENS, D), 1.0, 6.0, ((0, 8), (1, 4))),
        "key_vectors": gaussian(streams_of[1], (TOKENS, D), 1.0, 6.0, ((0, 8), (1, 4))),
        "value_vectors": gaussian(streams_of[2], (TOKENS, D), 1.0, 6.0, ((0, 8), (1, 4))),
        "level_weight": jnp.clip(jnp.exp(math.log(1.0) - 3.912023 * jax.random.uniform(streams_of[3], (TOKENS, HEADS * LEVELS), jnp.float32) ** level_of(streams_of[3], (TOKENS, HEADS * LEVELS), ((0, 8), (1, 4)), -0.2, 0.2)), 0.02, 1.0),
        "gate_values": gaussian(streams_of[4], (TOKENS, D), 1.0, 6.0, ((0, 32),)),
        "norm_gain": jnp.clip(1.0 + 0.1 * jax.random.normal(streams_of[5], (D,), jnp.float32), 0.5, 1.5),
    }


def bit_levels(count):
    indices = jnp.arange(count, dtype=jnp.int32)
    mixed = jnp.bitwise_xor(indices[:, None], indices[None, :])
    levels = jnp.zeros((count, count), jnp.int32)
    for height in range(count.bit_length() - 1):
        levels = levels + (mixed >= 1 << height).astype(jnp.int32)
    causal = indices[None, :] <= indices[:, None]
    return (levels, causal)

def local_attention(query_head, key_head, value_head, weight_head, levels, causal):
    scores = jnp.dot(query_head, key_head.T, preferred_element_type=jnp.float32)
    factor = jnp.zeros(scores.shape, jnp.float32)
    for height in range(query_head.shape[0].bit_length()):
        factor = factor + jnp.where(levels == height, weight_head[:, height:height + 1], jnp.float32(0.0))
    weighted = jnp.where(causal, scores * factor, jnp.float32(0.0)).astype(jnp.bfloat16)
    return jnp.dot(weighted, value_head, preferred_element_type=jnp.float32)

def reference(queries, key_vectors, value_vectors, level_weight, gate_values, norm_gain):
    width = HEADS * HEAD_DIM
    seq_bits = N_SEQ.bit_length() - 1
    local_bits = TOK_DEV.bit_length() - 1
    query_blocks = queries.reshape(N_SEQ, TOK_DEV, HEADS, HEAD_DIM)
    key_blocks = key_vectors.reshape(N_SEQ, TOK_DEV, HEADS, HEAD_DIM)
    value_blocks = value_vectors.reshape(N_SEQ, TOK_DEV, HEADS, HEAD_DIM)
    weight_blocks = level_weight.reshape(N_SEQ, TOK_DEV, HEADS, LEVELS)

    def state_of(inputs):
        return jnp.einsum('che,chf->hef', inputs[0].astype(jnp.float32), inputs[1].astype(jnp.float32), precision=lax.Precision.HIGHEST)
    states = lax.map(state_of, (key_blocks, value_blocks))
    left_sums = []
    for height in range(1, seq_bits + 1):
        span = 2 ** (height - 1)
        grouped = states.reshape(N_SEQ // (2 * span), 2, span, HEADS, HEAD_DIM, HEAD_DIM)
        left_sums.append(lax.optimization_barrier(jnp.sum(grouped[:, 0], axis=1)))
    levels, causal = bit_levels(TOK_DEV)

    def per_block(inputs):
        query_block, key_block, value_block, weight_block, position = inputs

        def per_head(head_inputs):
            return local_attention(head_inputs[0], head_inputs[1], head_inputs[2], head_inputs[3], levels, causal)
        inner = lax.map(per_head, (query_block.transpose(1, 0, 2), key_block.transpose(1, 0, 2), value_block.transpose(1, 0, 2), weight_block.transpose(1, 0, 2)))
        inner = inner.transpose(1, 0, 2)
        cross = jnp.zeros((TOK_DEV, HEADS, HEAD_DIM), jnp.float32)
        for height in range(1, seq_bits + 1):
            chosen = lax.dynamic_index_in_dim(left_sums[height - 1], jnp.right_shift(position, height).astype(jnp.int32), 0, keepdims=False)
            upper = (jnp.right_shift(position, height - 1) & 1).astype(jnp.float32)
            rounded = (chosen * upper).astype(jnp.bfloat16)
            term = jnp.einsum('che,hef->chf', query_block.astype(jnp.float32), rounded.astype(jnp.float32), precision=lax.Precision.HIGHEST)
            cross = cross + weight_block[:, :, local_bits + height, None] * term
        return (inner + cross).reshape(TOK_DEV, width).astype(jnp.bfloat16)
    attended = lax.map(per_block, (query_blocks, key_blocks, value_blocks, weight_blocks, jnp.arange(N_SEQ, dtype=jnp.int32)))
    attended = attended.reshape(N_SEQ * TOK_DEV, width).astype(jnp.float32)
    mean_square = lax.optimization_barrier(jnp.mean(attended * attended, axis=1, keepdims=True))
    gating = jax.nn.silu(gate_values.astype(jnp.float32))
    return (attended * lax.rsqrt(mean_square + 1e-06) * norm_gain[None, :] * gating).astype(jnp.bfloat16)
```

```python
import functools

import jax
import jax.numpy as jnp
from jax import lax
from jax.experimental import pallas as pl
from jax.experimental.pallas import tpu as pltpu
from jax.sharding import PartitionSpec as P

HEAD_DIM = 128
LEVELS = 16
CHUNK = 128
LANES = 128
SUB = 8
SUB_BITS = 3
GROUP = 2
PER_TILE = LANES // LEVELS
SIZES = (4, 4)
ORDER = (
    ("S", 0),
    ("S", 1),
    ("A", 0),
    ("S", 2),
    ("A", 0),
    ("A", 1),
    ("I", 0),
    ("F", 0),
    ("A", 1),
    ("A", 2),
    ("I", 1),
    ("F", 1),
    ("A", 2),
    ("I", 2),
    ("I", 2),
    ("F", 2),
    ("N", 0),
    ("N", 1),
    ("N", 2),
)
LONG = pl.CostEstimate(flops=3 * 10**9, bytes_accessed=10**6, transcendentals=0)


def dot(a, b, dims=((1,), (0,))):
    return lax.dot_general(a, b, (dims, ((), ())), preferred_element_type=jnp.float32)


def anywhere():
    return pl.BlockSpec(memory_space=pl.ANY)


def local():
    return pl.BlockSpec(memory_space=pltpu.VMEM)


def params(mebibytes):
    return pltpu.CompilerParams(vmem_limit_bytes=mebibytes * 1024 * 1024)


def hbm():
    return pl.BlockSpec(memory_space=pltpu.HBM)


def in_hbm(array):
    return pltpu.with_memory_space_constraint(array, pltpu.HBM)


def in_vmem(array):
    return pltpu.with_memory_space_constraint(array, pltpu.VMEM)


def fetches(source_ref, held_ref, first, heads, sems):
    copies = []
    for n in range(heads // GROUP):
        source = pl.ds((first + n * GROUP) * HEAD_DIM, GROUP * HEAD_DIM)
        target = pl.ds(n * GROUP * HEAD_DIM, GROUP * HEAD_DIM)
        copies.append(
            pltpu.make_async_copy(source_ref.at[:, source], held_ref.at[:, target], sems.at[n])
        )
    return copies


def state_kernel(first, heads, k_ref, v_ref, *refs):
    state_ref, rounded_ref, k_held, v_held, k_sems, v_sems = refs[-6:]
    k_copies = fetches(k_ref, k_held, first, heads, k_sems)
    v_copies = fetches(v_ref, v_held, first, heads, v_sems)
    for n in range(heads // GROUP):
        k_copies[n].start()
        v_copies[n].start()
    for n in range(heads // GROUP):
        k_copies[n].wait()
        v_copies[n].wait()
        for i in range(n * GROUP, (n + 1) * GROUP):
            here = slice(i * HEAD_DIM, (i + 1) * HEAD_DIM)
            state = dot(k_held[:, here], v_held[:, here], ((0,), (0,)))
            state_ref[i] = state
            rounded_ref[i] = state.astype(jnp.bfloat16)


def block_states(keys, values, first, heads, after):
    count = keys.shape[0]
    shape = (heads, HEAD_DIM, HEAD_DIM)
    held = jax.ShapeDtypeStruct((count, heads * HEAD_DIM), keys.dtype)
    return pl.pallas_call(
        functools.partial(state_kernel, first, heads),
        in_specs=[hbm(), hbm()] + [anywhere() for _ in after],
        out_specs=[local()] * 4,
        out_shape=[
            jax.ShapeDtypeStruct(shape, jnp.float32),
            jax.ShapeDtypeStruct(shape, jnp.bfloat16),
            held,
            held,
        ],
        scratch_shapes=[pltpu.SemaphoreType.DMA((heads // GROUP,))] * 2,
        compiler_params=params(8),
        cost_estimate=LONG,
        name="block_states",
    )(in_hbm(keys), in_hbm(values), *after)


def add_kernel(total_ref, held_ref, *refs):
    sum_ref, rounded_ref = refs[-2:]
    total = total_ref[...] + held_ref[...].astype(jnp.float32)
    sum_ref[...] = total
    rounded_ref[...] = total.astype(jnp.bfloat16)


def add_states(total, held, after):
    return pl.pallas_call(
        add_kernel,
        in_specs=[local()] * 2 + [anywhere() for _ in after],
        out_specs=[local(), local()],
        out_shape=[
            jax.ShapeDtypeStruct(total.shape, jnp.float32),
            jax.ShapeDtypeStruct(total.shape, jnp.bfloat16),
        ],
        compiler_params=params(8),
        cost_estimate=LONG,
        name="add_states",
    )(in_vmem(total), held, *after)


def factor_rows(weights, near_mix, far_mix):
    chunk = weights.shape[1]
    bits = chunk.bit_length() - 1
    row = [jnp.broadcast_to(weights[l : l + 1], (SUB, chunk)) for l in range(bits + 1)]
    near = row[0]
    for level in range(1, SUB_BITS + 1):
        near = jnp.where(near_mix >= 1 << (level - 1), row[level], near)
    near = jnp.where(near_mix >= SUB, jnp.float32(0.0), near)
    far = []
    for mix in far_mix:
        value = jnp.zeros((SUB, chunk), jnp.float32)
        for level in range(SUB_BITS + 1, bits + 1):
            value = jnp.where(mix >= 1 << (level - SUB_BITS - 1), row[level], value)
        far.append(value)
    return near, far


def inner_kernel(first, start, heads, q_source, k_ref, v_ref, w_ref, *refs):
    out_ref, q_ref, wt_ref, sems = refs[-4:]
    copies = fetches(q_source, q_ref, first, heads, sems)
    for copy in copies:
        copy.start()
    count = q_ref.shape[0]
    chunk = min(CHUNK, count)
    chunks = count // chunk
    chunk_bits = chunk.bit_length() - 1
    groups = chunk // SUB
    low_tile = first // PER_TILE
    tiles = (first + heads - 1) // PER_TILE + 1 - low_tile

    for tile in range(tiles):
        lanes = slice((low_tile + tile) * LANES, (low_tile + tile + 1) * LANES)
        for c in range(chunks):
            here = slice(c * chunk, (c + 1) * chunk)
            wt_ref[tile * LANES : (tile + 1) * LANES, here] = w_ref[here, lanes].T

    t = lax.broadcasted_iota(jnp.int32, (SUB, chunk), 1)
    s = lax.broadcasted_iota(jnp.int32, (SUB, chunk), 0)
    t_low, t_high = t & (SUB - 1), t >> SUB_BITS
    near_mix = jnp.where(s <= t_low, s ^ t_low, SUB)
    far_mix = []
    for a in range(max(1, groups // SUB)):
        s_high = s + SUB * a
        far_mix.append(jnp.where(t_high > s_high, t_high ^ s_high, 0))

    def group(step, carry):
        wide = GROUP * HEAD_DIM
        source = pl.ds(pl.multiple_of((first + step * GROUP) * HEAD_DIM, HEAD_DIM), wide)
        target = pl.ds(pl.multiple_of(step * wide, wide), wide)
        pltpu.make_async_copy(
            q_source.at[:, source], q_ref.at[:, target], sems.at[step]
        ).wait()
        head = first + step * GROUP
        lane = pl.multiple_of(head // PER_TILE * LANES, LANES)
        base = head % PER_TILE * LEVELS
        weights = pltpu.roll(w_ref[:, pl.ds(lane, LANES)], (LANES - base) % LANES, 1)
        rows_base = lane - low_tile * LANES + base
        sums = {}

        def columns(i, offset=0):
            place = (offset + step * GROUP + i) * HEAD_DIM
            return pl.ds(pl.multiple_of(place, HEAD_DIM), HEAD_DIM)

        def scores_of(i, c):
            here = slice(c * chunk, (c + 1) * chunk)
            held = columns(i, start)
            q, k, v = q_ref[here, columns(i)], k_ref[here, held], v_ref[here, held]
            scores = dot(k, q, ((1,), (1,)))
            terms = []
            for bit in range(chunks.bit_length() - 1):
                if c >> bit & 1:
                    terms.append((bit, dot(q, sums[i, bit].astype(jnp.bfloat16))))
            if c + 1 < chunks:
                state = dot(k, v, ((0,), (0,)))
                for bit in range(chunks.bit_length() - 1):
                    if not c >> bit & 1:
                        fresh = c % (1 << bit) == 0
                        sums[i, bit] = state if fresh else sums[i, bit] + state
            return scores, terms

        def store(i, c, scores, terms):
            here = slice(c * chunk, (c + 1) * chunk)
            own_rows = pl.ds(pl.multiple_of(rows_base + i * LEVELS, LEVELS), LEVELS)
            near, far = factor_rows(wt_ref[own_rows, here], near_mix, far_mix)
            parts = []
            for r in range(groups):
                line = jnp.broadcast_to(far[r // SUB][r % SUB : r % SUB + 1], (SUB, chunk))
                factor = jnp.where(t_high == r, near, line)
                parts.append(scores[r * SUB : (r + 1) * SUB] * factor)
            weighted = jnp.concatenate(parts, axis=0).astype(jnp.bfloat16)
            total = dot(weighted, v_ref[here, columns(i, start)], ((0,), (0,)))
            for bit, term in terms:
                level = i * LEVELS + chunk_bits + 1 + bit
                total += weights[here, level : level + 1] * term
            out_ref[here, columns(i)] = total

        waiting = []
        for i in range(GROUP):
            for c in range(chunks):
                waiting.append((i, c) + scores_of(i, c))
                if len(waiting) > 2:
                    store(*waiting.pop(0))
        for unit in waiting:
            store(*unit)
        return carry

    lax.fori_loop(0, heads // GROUP, group, 0)


def inner_part(queries, keys, values, weights, chunk_first, start, heads, after):
    count = queries.shape[0]
    first = chunk_first + start
    tiles = (first + heads - 1) // PER_TILE + 1 - first // PER_TILE
    shape = (count, heads * HEAD_DIM)
    return pl.pallas_call(
        functools.partial(inner_kernel, first, start, heads),
        in_specs=[hbm()] + [local()] * 3 + [anywhere() for _ in after],
        out_specs=[local()] * 2,
        out_shape=[
            jax.ShapeDtypeStruct(shape, jnp.float32),
            jax.ShapeDtypeStruct(shape, queries.dtype),
        ],
        scratch_shapes=[
            pltpu.VMEM((tiles * LANES, count), jnp.float32),
            pltpu.SemaphoreType.DMA((heads // GROUP,)),
        ],
        compiler_params=params(8),
        cost_estimate=LONG,
        name="inner_part",
    )(in_hbm(queries), in_vmem(keys), in_vmem(values), weights, *after)


def finish_kernel(first, start, heads, pairs, levels, place_ref, q_ref, w_ref, inner_ref, *refs):
    tiers = refs[:levels]
    outs = refs[len(refs) - 2 * len(pairs) :]
    count = q_ref.shape[0]
    rows = outs[0].shape[0]
    local_bits = count.bit_length() - 1
    flip = (place_ref[0] & 1) == 1

    def group(step, carry):
        head = first + step * GROUP
        lane = pl.multiple_of(head // PER_TILE * LANES, LANES)
        base = head % PER_TILE * LEVELS
        for n, pair in enumerate(pairs):
            spot = jnp.bitwise_xor(jnp.right_shift(place_ref[0], 1), pair)
            here = pl.ds(pl.multiple_of(spot * (2 * rows), 2 * rows), 2 * rows)
            weights = pltpu.roll(w_ref[here, pl.ds(lane, LANES)], (LANES - base) % LANES, 1)
            for i in range(GROUP):
                cols = pl.ds(pl.multiple_of((step * GROUP + i) * HEAD_DIM, HEAD_DIM), HEAD_DIM)
                q = q_ref[here, cols]
                total = inner_ref[here, cols]
                for m in range(levels):
                    level = i * LEVELS + local_bits + 1 + m
                    held = place_ref[1 + m].astype(jnp.float32)
                    tier = tiers[m][start + step * GROUP + i]
                    total += (weights[:, level : level + 1] * held) * dot(q, tier)
                upper, lower = total[:rows], total[rows:]
                outs[2 * n][:, cols] = jnp.where(flip, lower, upper).astype(jnp.bfloat16)
                outs[2 * n + 1][:, cols] = jnp.where(flip, upper, lower).astype(jnp.bfloat16)
        return carry

    lax.fori_loop(0, heads // GROUP, group, 0)


def finish(place, tiers, queries, inner, weights, chunk_first, start, heads, pairs, parts, after):
    rows = queries.shape[0] // parts
    outs = 2 * len(pairs)
    return pl.pallas_call(
        functools.partial(
            finish_kernel, chunk_first + start, start, heads, tuple(pairs), len(tiers)
        ),
        in_specs=[pl.BlockSpec(memory_space=pltpu.SMEM)]
        + [local()] * (3 + len(tiers))
        + [anywhere() for _ in after],
        out_specs=[local()] * outs,
        out_shape=[
            jax.ShapeDtypeStruct((rows, heads * HEAD_DIM), jnp.bfloat16) for _ in range(outs)
        ],
        compiler_params=params(8),
        cost_estimate=LONG,
        name="finish",
    )(place, queries, weights, inner, *tiers, *after)


def norm_kernel(layout, width, place_ref, gain_ref, gate_ref, *refs):
    out_ref = refs[-1]
    pieces = refs[:-1]
    tile = out_ref.shape[0]
    rows = pl.ds(pl.multiple_of(pl.program_id(0) * tile, tile), tile)
    square = None
    for ref in pieces:
        x = ref[rows, :].astype(jnp.float32)
        part = jnp.sum(x * x, axis=1, keepdims=True)
        square = part if square is None else square + part
    scale = lax.rsqrt(square / out_ref.shape[1] + 1e-06)
    for (step, start), ref in zip(layout, pieces):
        offset = pl.multiple_of(jnp.bitwise_xor(place_ref[0], step) * width + start, LANES)
        here = pl.ds(offset, ref.shape[1])
        half = gate_ref[rows, here].astype(jnp.float32) * 0.5
        gating = half + half * jnp.tanh(half)
        x = ref[rows, :].astype(jnp.float32) * scale
        out_ref[:, here] = (x * gain_ref[:, here] * gating).astype(jnp.bfloat16)


def normalize(place, gain, gate, layout, pieces, width):
    rows, features = gate.shape
    tile = min(64, rows)
    return pl.pallas_call(
        functools.partial(norm_kernel, layout, width),
        grid=(rows // tile,),
        in_specs=[pl.BlockSpec(memory_space=pltpu.SMEM)] + [local()] * (2 + len(pieces)),
        out_specs=pl.BlockSpec((tile, features), lambda i: (i, 0)),
        out_shape=jax.ShapeDtypeStruct((rows, features), jnp.bfloat16),
        compiler_params=params(8),
        cost_estimate=LONG,
        name="normalize",
    )(place, gain.reshape(1, features), gate, *pieces)


def cut(heads):
    sizes = []
    for size in SIZES:
        if heads - sum(sizes) > size:
            sizes.append(size)
    return sizes + [heads - sum(sizes)]


def per_device(queries, key_vectors, value_vectors, level_weight, gate_values, norm_gain):
    count, width = queries.shape
    heads = width // HEAD_DIM
    blocks = lax.axis_size("seq")
    parts = lax.axis_size("head")
    seq_bits = blocks.bit_length() - 1
    block = lax.axis_index("seq")
    flags = [jnp.right_shift(block, m) & 1 for m in range(seq_bits)]
    place = jnp.stack([lax.axis_index("head")] + flags).astype(jnp.int32)

    sizes = cut(heads)
    chunks = range(len(sizes))
    firsts = [sum(sizes[:g]) for g in chunks]

    inner_sizes = []
    for size in sizes:
        inner_sizes.append([min(4, size - start) for start in range(0, size, 4)])

    totals, sends, tiers, inner, keys, values = {}, {}, {}, {}, {}, {}
    pieces, layout = [], []
    last = {}

    def hop(g):
        m = len(tiers[g])
        pairs = [(i, i ^ 1 << m) for i in range(blocks)]
        tiers[g].append(lax.ppermute(sends[g], "seq", pairs))

    def state_step(g):
        totals[g], sends[g], keys[g], values[g] = block_states(
            key_vectors, value_vectors, firsts[g], sizes[g], tuple(last.values())
        )
        tiers[g] = []
        last["kernel"] = sends[g]
        hop(g)

    def add_step(g):
        if len(tiers[g]) < seq_bits:
            totals[g], sends[g] = add_states(totals[g], tiers[g][-1], tuple(last.values()))
            last["kernel"] = sends[g]
            hop(g)

    def inner_step(g):
        done = inner.setdefault(g, [])
        if len(done) < len(inner_sizes[g]):
            start = sum(inner_sizes[g][: len(done)])
            done.append(
                inner_part(
                    queries,
                    keys[g],
                    values[g],
                    level_weight,
                    firsts[g],
                    start,
                    inner_sizes[g][len(done)],
                    tuple(last.values()),
                )
            )
            last["kernel"] = done[-1][0]

    def finish_step(g, pairs):
        start = 0
        for (part, q_part), size in zip(inner[g], inner_sizes[g]):
            outs = finish(
                place,
                tiers[g],
                q_part,
                part,
                level_weight,
                firsts[g],
                start,
                size,
                pairs,
                parts,
                tuple(last.values()),
            )
            last["kernel"] = outs[-1]
            for offset, out in enumerate(outs):
                step = 2 * pairs[0] + offset
                if step:
                    out = lax.ppermute(out, "head", [(i, i ^ step) for i in range(parts)])
                pieces.append(out)
                layout.append((step, (firsts[g] + start) * HEAD_DIM))
            start += size

    far, near = range(1, parts // 2), range(1)
    for kind, g in ORDER:
        if g >= len(sizes):
            continue
        if kind == "S":
            state_step(g)
        if kind == "A":
            add_step(g)
        if kind == "I":
            inner_step(g)
        if kind == "F":
            for _ in range(seq_bits):
                add_step(g)
            finish_step(g, far)
        if kind == "N":
            finish_step(g, near)
    return normalize(place, norm_gain, gate_values, layout, pieces, width)


def solution(mesh):
    placed = (
        P("seq", "head"),
        P("seq", "head"),
        P("seq", "head"),
        P("seq", "head"),
        P(("seq", "head"), None),
        P(),
    )
    return jax.shard_map(
        per_device, mesh=mesh, in_specs=placed, out_specs=P(("seq", "head"), None), check_vma=False
    )
```

```python
import functools

import jax
import jax.numpy as jnp
from jax import lax
from jax.experimental import pallas as pl
from jax.experimental.pallas import tpu as pltpu
from jax.sharding import PartitionSpec as P

HEAD_DIM = 128
LEVELS = 16
CHUNK = 128
LANES = 128
SUB = 8
SUB_BITS = 3
GROUP = 2
PER_TILE = LANES // LEVELS
SIZES = (4, 4)
ORDER = (
    ("S", 0),
    ("S", 1),
    ("A", 0),
    ("S", 2),
    ("A", 0),
    ("A", 1),
    ("I", 0),
    ("A", 2),
    ("F", 0),
    ("A", 1),
    ("I", 1),
    ("A", 2),
    ("F", 1),
    ("I", 2),
    ("N", 0),
    ("F", 2),
    ("N", 1),
    ("N", 2),
)
TINY = pl.CostEstimate(flops=1024, bytes_accessed=1024, transcendentals=0)
LONG = pl.CostEstimate(flops=3 * 10**9, bytes_accessed=10**6, transcendentals=0)


def dot(a, b, dims=((1,), (0,))):
    return lax.dot_general(a, b, (dims, ((), ())), preferred_element_type=jnp.float32)


def anywhere():
    return pl.BlockSpec(memory_space=pl.ANY)


def cost(pairs):
    return LONG if pairs[0] else TINY


def local():
    return pl.BlockSpec(memory_space=pltpu.VMEM)


def params(mebibytes):
    return pltpu.CompilerParams(vmem_limit_bytes=mebibytes * 1024 * 1024)


def hbm():
    return pl.BlockSpec(memory_space=pltpu.HBM)


def in_hbm(array):
    return pltpu.with_memory_space_constraint(array, pltpu.HBM)


def in_vmem(array):
    return pltpu.with_memory_space_constraint(array, pltpu.VMEM)


def fetches(source_ref, held_ref, first, heads, sems):
    copies = []
    for n in range(heads // GROUP):
        source = pl.ds((first + n * GROUP) * HEAD_DIM, GROUP * HEAD_DIM)
        target = pl.ds(n * GROUP * HEAD_DIM, GROUP * HEAD_DIM)
        copies.append(
            pltpu.make_async_copy(source_ref.at[:, source], held_ref.at[:, target], sems.at[n])
        )
    return copies


def state_kernel(first, heads, k_ref, v_ref, *refs):
    rounded_ref, k_held, v_held, k_sems, v_sems = refs[-5:]
    k_copies = fetches(k_ref, k_held, first, heads, k_sems)
    v_copies = fetches(v_ref, v_held, first, heads, v_sems)
    for n in range(heads // GROUP):
        k_copies[n].start()
        v_copies[n].start()
    for n in range(heads // GROUP):
        k_copies[n].wait()
        v_copies[n].wait()
        for i in range(n * GROUP, (n + 1) * GROUP):
            here = slice(i * HEAD_DIM, (i + 1) * HEAD_DIM)
            state = dot(k_held[:, here], v_held[:, here], ((0,), (0,)))
            rounded_ref[i] = state.astype(jnp.bfloat16)


def block_states(keys, values, first, heads, after):
    held = pltpu.VMEM((keys.shape[0], heads * HEAD_DIM), keys.dtype)
    return pl.pallas_call(
        functools.partial(state_kernel, first, heads),
        in_specs=[hbm(), hbm()] + [anywhere() for _ in after],
        out_specs=local(),
        out_shape=jax.ShapeDtypeStruct((heads, HEAD_DIM, HEAD_DIM), jnp.bfloat16),
        scratch_shapes=[held, held] + [pltpu.SemaphoreType.DMA((heads // GROUP,))] * 2,
        compiler_params=params(12),
        cost_estimate=LONG,
        name="block_states",
    )(in_hbm(keys), in_hbm(values), *after)


def add_kernel(total_ref, held_ref, *refs):
    sum_ref = refs[-1]
    total = total_ref[...].astype(jnp.float32) + held_ref[...].astype(jnp.float32)
    sum_ref[...] = total.astype(jnp.bfloat16)


def add_states(total, held, after):
    return pl.pallas_call(
        add_kernel,
        in_specs=[local()] * 2 + [anywhere() for _ in after],
        out_specs=local(),
        out_shape=jax.ShapeDtypeStruct(total.shape, jnp.bfloat16),
        compiler_params=params(4),
        cost_estimate=LONG,
        name="add_states",
    )(in_vmem(total), held, *after)


def factor_rows(weights, near_mix, far_mix):
    chunk = weights.shape[1]
    bits = chunk.bit_length() - 1
    row = [jnp.broadcast_to(weights[l : l + 1], (SUB, chunk)) for l in range(bits + 1)]
    near = row[0]
    for level in range(1, SUB_BITS + 1):
        near = jnp.where(near_mix >= 1 << (level - 1), row[level], near)
    near = jnp.where(near_mix >= SUB, jnp.float32(0.0), near)
    far = []
    for mix in far_mix:
        value = jnp.zeros((SUB, chunk), jnp.float32)
        for level in range(SUB_BITS + 1, bits + 1):
            value = jnp.where(mix >= 1 << (level - SUB_BITS - 1), row[level], value)
        far.append(value)
    return near, far


def inner_kernel(
    first, heads, pairs, rows, place_ref, q_source, k_source, v_source, w_ref, *refs
):
    out_ref, q_ref, k_ref, v_ref, wt_ref, sems, kv_sems = refs[-7:]
    wide = GROUP * HEAD_DIM
    spots = [jnp.bitwise_xor(jnp.right_shift(place_ref[0], 1), pair) for pair in pairs]

    def fetch(step, n):
        source = pl.ds(pl.multiple_of((first + step * GROUP) * HEAD_DIM, HEAD_DIM), wide)
        target = pl.ds(pl.multiple_of(step * wide, wide), wide)
        above = pl.ds(pl.multiple_of(spots[n] * rows, rows), rows)
        return pltpu.make_async_copy(
            q_source.at[above, source],
            q_ref.at[n * rows : (n + 1) * rows, target],
            sems.at[n, step],
        )

    def fetch_whole(step, m):
        source = pl.ds(pl.multiple_of((first + step * GROUP) * HEAD_DIM, HEAD_DIM), wide)
        target = pl.ds(pl.multiple_of(step * wide, wide), wide)
        return pltpu.make_async_copy(
            (k_source, v_source)[m].at[:, source],
            (k_ref, v_ref)[m].at[:, target],
            kv_sems.at[m, step],
        )

    for step in range(heads // GROUP):
        for m in range(2):
            fetch_whole(step, m).start()
        for n in range(len(pairs)):
            fetch(step, n).start()
    count = k_ref.shape[0]
    chunk = min(CHUNK, rows)
    chunks = rows // chunk
    chunk_bits = chunk.bit_length() - 1
    row_bits = rows.bit_length() - 1
    blocks = count // rows
    groups = chunk // SUB
    low_tile = first // PER_TILE
    tiles = (first + heads - 1) // PER_TILE + 1 - low_tile

    def span(n, c):
        return pl.ds(pl.multiple_of(spots[n] * rows + c * chunk, chunk), chunk)

    for tile in range(tiles):
        lanes = slice((low_tile + tile) * LANES, (low_tile + tile + 1) * LANES)
        for n in range(len(pairs)):
            for c in range(chunks):
                here = slice(n * rows + c * chunk, n * rows + (c + 1) * chunk)
                wt_ref[tile * LANES : (tile + 1) * LANES, here] = w_ref[span(n, c), lanes].T

    t = lax.broadcasted_iota(jnp.int32, (SUB, chunk), 1)
    s = lax.broadcasted_iota(jnp.int32, (SUB, chunk), 0)
    t_low, t_high = t & (SUB - 1), t >> SUB_BITS
    near_mix = jnp.where(s <= t_low, s ^ t_low, SUB)
    far_mix = []
    for a in range(max(1, groups // SUB)):
        s_high = s + SUB * a
        far_mix.append(jnp.where(t_high > s_high, t_high ^ s_high, 0))

    def group(step, carry):
        for m in range(2):
            fetch_whole(step, m).wait()
        for n in range(len(pairs)):
            fetch(step, n).wait()
        head = first + step * GROUP
        lane = pl.multiple_of(head // PER_TILE * LANES, LANES)
        base = head % PER_TILE * LEVELS
        rows_base = lane - low_tile * LANES + base
        shift = (LANES - base) % LANES
        weights = []
        for n in range(len(pairs)):
            above = pl.ds(pl.multiple_of(spots[n] * rows, rows), rows)
            weights.append(pltpu.roll(w_ref[above, pl.ds(lane, LANES)], shift, 1))
        sums, outer = {}, {}

        def columns(i):
            place = (step * GROUP + i) * HEAD_DIM
            return pl.ds(pl.multiple_of(place, HEAD_DIM), HEAD_DIM)

        def outer_tiers(i):
            held = columns(i)
            states = []
            for block in range(blocks - 1):
                here = slice(block * rows, (block + 1) * rows)
                states.append(dot(k_ref[here, held], v_ref[here, held], ((0,), (0,))))
            for n, spot in enumerate(spots):
                for bit in range(blocks.bit_length() - 1):
                    tier = jnp.zeros((HEAD_DIM, HEAD_DIM), jnp.float32)
                    for block, state in enumerate(states):
                        if not block >> bit & 1:
                            same = jnp.right_shift(spot, bit + 1) == block >> (bit + 1)
                            upper = (jnp.right_shift(spot, bit) & 1) == 1
                            tier += jnp.where(same & upper, state, jnp.float32(0.0))
                    outer[i, n, bit] = tier.astype(jnp.bfloat16)

        def scores_of(i, n, c):
            held = columns(i)
            here = slice(n * rows + c * chunk, n * rows + (c + 1) * chunk)
            q, k, v = q_ref[here, columns(i)], k_ref[span(n, c), held], v_ref[span(n, c), held]
            scores = dot(k, q, ((1,), (1,)))
            terms = []
            for bit in range(chunks.bit_length() - 1):
                if c >> bit & 1:
                    tier = sums[i, n, bit].astype(jnp.bfloat16)
                    terms.append((chunk_bits + 1 + bit, dot(q, tier)))
            for bit in range(blocks.bit_length() - 1):
                terms.append((row_bits + 1 + bit, dot(q, outer[i, n, bit])))
            if c + 1 < chunks:
                state = dot(k, v, ((0,), (0,)))
                for bit in range(chunks.bit_length() - 1):
                    if not c >> bit & 1:
                        fresh = c % (1 << bit) == 0
                        sums[i, n, bit] = state if fresh else sums[i, n, bit] + state
            return scores, terms

        def store(i, n, c, scores, terms):
            here = slice(n * rows + c * chunk, n * rows + (c + 1) * chunk)
            own_rows = pl.ds(pl.multiple_of(rows_base + i * LEVELS, LEVELS), LEVELS)
            near, far = factor_rows(wt_ref[own_rows, here], near_mix, far_mix)
            parts = []
            for r in range(groups):
                line = jnp.broadcast_to(far[r // SUB][r % SUB : r % SUB + 1], (SUB, chunk))
                factor = jnp.where(t_high == r, near, line)
                parts.append(scores[r * SUB : (r + 1) * SUB] * factor)
            weighted = jnp.concatenate(parts, axis=0).astype(jnp.bfloat16)
            total = dot(weighted, v_ref[span(n, c), columns(i)], ((0,), (0,)))
            for level, term in terms:
                column = i * LEVELS + level
                scale = weights[n][c * chunk : (c + 1) * chunk, column : column + 1]
                total += scale * term
            out_ref[here, columns(i)] = total

        waiting = []
        for i in range(GROUP):
            outer_tiers(i)
            for n in range(len(pairs)):
                for c in range(chunks):
                    waiting.append((i, n, c) + scores_of(i, n, c))
                    if len(waiting) > 2:
                        store(*waiting.pop(0))
        for unit in waiting:
            store(*unit)
        return carry

    lax.fori_loop(0, heads // GROUP, group, 0)


def inner_part(
    place, queries, keys, values, weights, chunk_first, start, heads, pairs, parts, after
):
    rows = 2 * queries.shape[0] // parts
    first = chunk_first + start
    tiles = (first + heads - 1) // PER_TILE + 1 - first // PER_TILE
    shape = (len(pairs) * rows, heads * HEAD_DIM)
    return pl.pallas_call(
        functools.partial(inner_kernel, first, heads, tuple(pairs), rows),
        in_specs=[pl.BlockSpec(memory_space=pltpu.SMEM), hbm(), hbm(), hbm(), local()]
        + [anywhere() for _ in after],
        out_specs=[local()] * 2,
        out_shape=[
            jax.ShapeDtypeStruct(shape, jnp.float32),
            jax.ShapeDtypeStruct(shape, queries.dtype),
        ],
        scratch_shapes=[
            pltpu.VMEM((queries.shape[0], shape[1]), keys.dtype),
            pltpu.VMEM((queries.shape[0], shape[1]), values.dtype),
            pltpu.VMEM((tiles * LANES, shape[0]), jnp.float32),
            pltpu.SemaphoreType.DMA((len(pairs), heads // GROUP)),
            pltpu.SemaphoreType.DMA((2, heads // GROUP)),
        ],
        compiler_params=params(12),
        cost_estimate=cost(pairs),
        name="inner_part",
    )(place, in_hbm(queries), in_hbm(keys), in_hbm(values), weights, *after)


def finish_kernel(first, start, heads, pairs, levels, place_ref, q_ref, w_ref, inner_ref, *refs):
    tiers = refs[:levels]
    outs = refs[len(refs) - 2 * len(pairs) :]
    local_bits = w_ref.shape[0].bit_length() - 1
    rows = outs[0].shape[0]
    flip = (place_ref[0] & 1) == 1

    def group(step, carry):
        head = first + step * GROUP
        lane = pl.multiple_of(head // PER_TILE * LANES, LANES)
        base = head % PER_TILE * LEVELS
        for n, pair in enumerate(pairs):
            spot = jnp.bitwise_xor(jnp.right_shift(place_ref[0], 1), pair)
            here = pl.ds(pl.multiple_of(spot * (2 * rows), 2 * rows), 2 * rows)
            weights = pltpu.roll(w_ref[here, pl.ds(lane, LANES)], (LANES - base) % LANES, 1)
            for i in range(GROUP):
                cols = pl.ds(pl.multiple_of((step * GROUP + i) * HEAD_DIM, HEAD_DIM), HEAD_DIM)
                own = slice(2 * n * rows, 2 * (n + 1) * rows)
                q = q_ref[own, cols]
                total = inner_ref[own, cols]
                for m in range(levels):
                    level = i * LEVELS + local_bits + 1 + m
                    held = place_ref[1 + m].astype(jnp.float32)
                    tier = tiers[m][start + step * GROUP + i]
                    total += (weights[:, level : level + 1] * held) * dot(q, tier)
                upper, lower = total[:rows], total[rows:]
                outs[2 * n][:, cols] = jnp.where(flip, lower, upper).astype(jnp.bfloat16)
                outs[2 * n + 1][:, cols] = jnp.where(flip, upper, lower).astype(jnp.bfloat16)
        return carry

    lax.fori_loop(0, heads // GROUP, group, 0)


def finish(place, tiers, queries, inner, weights, chunk_first, start, heads, pairs, parts, after):
    rows = weights.shape[0] // parts
    outs = 2 * len(pairs)
    return pl.pallas_call(
        functools.partial(
            finish_kernel, chunk_first + start, start, heads, tuple(pairs), len(tiers)
        ),
        in_specs=[pl.BlockSpec(memory_space=pltpu.SMEM)]
        + [local()] * (3 + len(tiers))
        + [anywhere() for _ in after],
        out_specs=[local()] * outs,
        out_shape=[
            jax.ShapeDtypeStruct((rows, heads * HEAD_DIM), jnp.bfloat16) for _ in range(outs)
        ],
        compiler_params=params(8),
        cost_estimate=cost(pairs),
        name="finish",
    )(place, queries, weights, inner, *tiers, *after)


def gate_kernel(gain_ref, gate_ref, *refs):
    out_ref = refs[-1]
    tile = min(LANES * SUB, out_ref.shape[1])

    def columns(j, carry):
        here = pl.ds(pl.multiple_of(j * tile, tile), tile)
        half = gate_ref[:, here].astype(jnp.float32) * 0.5
        out_ref[:, here] = (half + half * jnp.tanh(half)) * gain_ref[:, here]
        return carry

    lax.fori_loop(0, out_ref.shape[1] // tile, columns, 0)


def gating(gain, gate, after):
    return pl.pallas_call(
        gate_kernel,
        in_specs=[local()] * 2 + [anywhere() for _ in after],
        out_specs=local(),
        out_shape=jax.ShapeDtypeStruct(gate.shape, jnp.float32),
        compiler_params=params(8),
        cost_estimate=TINY,
        name="gating",
    )(gain.reshape(1, gain.shape[0]), gate, *after)


def norm_kernel(layout, width, place_ref, gating_ref, *refs):
    out_ref = refs[-1]
    pieces = refs[:-1]
    tile = out_ref.shape[0]
    rows = pl.ds(pl.multiple_of(pl.program_id(0) * tile, tile), tile)
    square = None
    for ref in pieces:
        x = ref[rows, :].astype(jnp.float32)
        part = jnp.sum(x * x, axis=1, keepdims=True)
        square = part if square is None else square + part
    scale = lax.rsqrt(square / out_ref.shape[1] + 1e-06)
    for (step, start), ref in zip(layout, pieces):
        offset = pl.multiple_of(jnp.bitwise_xor(place_ref[0], step) * width + start, LANES)
        here = pl.ds(offset, ref.shape[1])
        x = ref[rows, :].astype(jnp.float32) * scale
        out_ref[:, here] = (x * gating_ref[rows, here]).astype(jnp.bfloat16)


def normalize(place, gated, layout, pieces, width):
    rows, features = gated.shape
    tile = min(64, rows)
    return pl.pallas_call(
        functools.partial(norm_kernel, layout, width),
        grid=(rows // tile,),
        in_specs=[pl.BlockSpec(memory_space=pltpu.SMEM)] + [local()] * (1 + len(pieces)),
        out_specs=pl.BlockSpec((tile, features), lambda i: (i, 0)),
        out_shape=jax.ShapeDtypeStruct((rows, features), jnp.bfloat16),
        compiler_params=params(8),
        cost_estimate=LONG,
        name="normalize",
    )(place, in_vmem(gated), *pieces)


def cut(heads):
    sizes = []
    for size in SIZES:
        if heads - sum(sizes) > size:
            sizes.append(size)
    return sizes + [heads - sum(sizes)]


def per_device(queries, key_vectors, value_vectors, level_weight, gate_values, norm_gain):
    count, width = queries.shape
    heads = width // HEAD_DIM
    blocks = lax.axis_size("seq")
    parts = lax.axis_size("head")
    seq_bits = blocks.bit_length() - 1
    block = lax.axis_index("seq")
    flags = [jnp.right_shift(block, m) & 1 for m in range(seq_bits)]
    place = jnp.stack([lax.axis_index("head")] + flags).astype(jnp.int32)

    sizes = cut(heads)
    chunks = range(len(sizes))
    firsts = [sum(sizes[:g]) for g in chunks]

    sends, tiers, inner = {}, {}, {}
    pieces, layout, arrived = [], [], {}
    last = {}

    def hop(g):
        m = len(tiers[g])
        pairs = [(i, i ^ 1 << m) for i in range(blocks)]
        tiers[g].append(lax.ppermute(sends[g], "seq", pairs))

    def state_step(g):
        sends[g] = block_states(
            key_vectors, value_vectors, firsts[g], sizes[g], tuple(last.values())
        )
        tiers[g] = []
        last["kernel"] = sends[g]
        hop(g)

    def add_step(g):
        if len(tiers[g]) < seq_bits:
            sends[g] = add_states(sends[g], tiers[g][-1], tuple(last.values()))
            last["kernel"] = sends[g]
            hop(g)

    def inner_step(g, pairs, start, size):
        inner[g] = inner_part(
            place,
            queries,
            key_vectors,
            value_vectors,
            level_weight,
            firsts[g],
            start,
            size,
            pairs,
            parts,
            tuple(last.values()),
        )
        last["kernel"] = inner[g][0]

    def finish_step(g, pairs, start, size):
        part, q_part = inner[g]
        behind = g - 2 if pairs[0] else g - 1 if g == len(sizes) - 1 else -1
        before = tuple(arrived.get(behind, ()))
        outs = finish(
            place,
            tiers[g],
            q_part,
            part,
            level_weight,
            firsts[g],
            start,
            size,
            pairs,
            parts,
            tuple(last.values()) + before,
        )
        last["kernel"] = outs[-1]
        for step, out in enumerate(outs, 2 * pairs[0]):
            if step:
                out = lax.ppermute(out, "head", [(i, i ^ step) for i in range(parts)])
            pieces.append(out)
            layout.append((step, (firsts[g] + start) * HEAD_DIM))
            if pairs[0]:
                arrived.setdefault(g, []).append(out)

    far, near = range(1, parts // 2), range(1)
    for kind, g in ORDER:
        if g >= len(sizes):
            continue
        if kind == "S":
            state_step(g)
        if kind == "A":
            add_step(g)
        if kind == "I":
            inner_step(g, far, 0, sizes[g])
        if kind == "F":
            for _ in range(seq_bits):
                add_step(g)
            finish_step(g, far, 0, sizes[g])
        if kind == "N":
            for start in range(0, sizes[g], SIZES[0]):
                size = min(SIZES[0], sizes[g] - start)
                inner_step(g, near, start, size)
                finish_step(g, near, start, size)
    gated = gating(norm_gain, gate_values, tuple(last.values()))
    return normalize(place, gated, layout, pieces, width)


def solution(mesh):
    placed = (
        P("seq", "head"),
        P("seq", "head"),
        P("seq", "head"),
        P("seq", "head"),
        P(("seq", "head"), None),
        P(),
    )
    return jax.shard_map(
        per_device, mesh=mesh, in_specs=placed, out_specs=P(("seq", "head"), None), check_vma=False
    )
```

```python
import functools

import jax
import jax.numpy as jnp
from jax import lax
from jax.experimental import pallas as pl
from jax.experimental.pallas import tpu as pltpu
from jax.sharding import PartitionSpec as P

HEAD_DIM = 128
LEVELS = 16
CHUNK = 128
LANES = 128
SUB = 8
SUB_BITS = 3
GROUP = 2
PER_TILE = LANES // LEVELS
SIZES = (4, 4)
ORDER = (
    ("S", 0),
    ("S", 1),
    ("A", 0),
    ("S", 2),
    ("A", 0),
    ("A", 1),
    ("I", 0),
    ("A", 2),
    ("F", 0),
    ("A", 1),
    ("W", 1),
    ("A", 2),
    ("F", 1),
    ("I", 2),
    ("N", 1),
    ("F", 2),
    ("N", 0),
    ("N", 2),
)
TINY = pl.CostEstimate(flops=1024, bytes_accessed=1024, transcendentals=0)
LONG = pl.CostEstimate(flops=3 * 10**9, bytes_accessed=10**6, transcendentals=0)


def dot(a, b, dims=((1,), (0,))):
    return lax.dot_general(a, b, (dims, ((), ())), preferred_element_type=jnp.float32)


def anywhere():
    return pl.BlockSpec(memory_space=pl.ANY)


def cost(pairs):
    return LONG if pairs[0] else TINY


def local():
    return pl.BlockSpec(memory_space=pltpu.VMEM)


def params(mebibytes):
    return pltpu.CompilerParams(vmem_limit_bytes=mebibytes * 1024 * 1024)


def hbm():
    return pl.BlockSpec(memory_space=pltpu.HBM)


def in_hbm(array):
    return pltpu.with_memory_space_constraint(array, pltpu.HBM)


def in_vmem(array):
    return pltpu.with_memory_space_constraint(array, pltpu.VMEM)


def fetches(source_ref, held_ref, first, heads, sems):
    copies = []
    for n in range(heads // GROUP):
        source = pl.ds((first + n * GROUP) * HEAD_DIM, GROUP * HEAD_DIM)
        target = pl.ds(n * GROUP * HEAD_DIM, GROUP * HEAD_DIM)
        copies.append(
            pltpu.make_async_copy(source_ref.at[:, source], held_ref.at[:, target], sems.at[n])
        )
    return copies


def state_kernel(first, heads, k_ref, v_ref, *refs):
    rounded_ref, k_held, v_held, k_sems, v_sems = refs[-5:]
    k_copies = fetches(k_ref, k_held, first, heads, k_sems)
    v_copies = fetches(v_ref, v_held, first, heads, v_sems)
    for n in range(heads // GROUP):
        k_copies[n].start()
        v_copies[n].start()
    for n in range(heads // GROUP):
        k_copies[n].wait()
        v_copies[n].wait()
        for i in range(n * GROUP, (n + 1) * GROUP):
            here = slice(i * HEAD_DIM, (i + 1) * HEAD_DIM)
            state = dot(k_held[:, here], v_held[:, here], ((0,), (0,)))
            rounded_ref[i] = state.astype(jnp.bfloat16)


def block_states(keys, values, first, heads, after):
    held = pltpu.VMEM((keys.shape[0], heads * HEAD_DIM), keys.dtype)
    return pl.pallas_call(
        functools.partial(state_kernel, first, heads),
        in_specs=[hbm(), hbm()] + [anywhere() for _ in after],
        out_specs=local(),
        out_shape=jax.ShapeDtypeStruct((heads, HEAD_DIM, HEAD_DIM), jnp.bfloat16),
        scratch_shapes=[held, held] + [pltpu.SemaphoreType.DMA((heads // GROUP,))] * 2,
        compiler_params=params(12),
        cost_estimate=LONG,
        name="block_states",
    )(in_hbm(keys), in_hbm(values), *after)


def add_kernel(total_ref, held_ref, *refs):
    sum_ref = refs[-1]
    total = total_ref[...].astype(jnp.float32) + held_ref[...].astype(jnp.float32)
    sum_ref[...] = total.astype(jnp.bfloat16)


def add_states(total, held, after):
    return pl.pallas_call(
        add_kernel,
        in_specs=[local()] * 2 + [anywhere() for _ in after],
        out_specs=local(),
        out_shape=jax.ShapeDtypeStruct(total.shape, jnp.bfloat16),
        compiler_params=params(4),
        cost_estimate=LONG,
        name="add_states",
    )(in_vmem(total), held, *after)


def factor_rows(weights, near_mix, far_mix):
    chunk = weights.shape[1]
    bits = chunk.bit_length() - 1
    row = [jnp.broadcast_to(weights[l : l + 1], (SUB, chunk)) for l in range(bits + 1)]
    near = row[0]
    for level in range(1, SUB_BITS + 1):
        near = jnp.where(near_mix >= 1 << (level - 1), row[level], near)
    near = jnp.where(near_mix >= SUB, jnp.float32(0.0), near)
    far = []
    for mix in far_mix:
        value = jnp.zeros((SUB, chunk), jnp.float32)
        for level in range(SUB_BITS + 1, bits + 1):
            value = jnp.where(mix >= 1 << (level - SUB_BITS - 1), row[level], value)
        far.append(value)
    return near, far


def inner_kernel(
    first, heads, pairs, rows, place_ref, q_source, k_source, v_source, w_ref, *refs
):
    out_ref, q_ref, k_ref, v_ref, wt_ref, sems, kv_sems = refs[-7:]
    wide = GROUP * HEAD_DIM
    spots = [jnp.bitwise_xor(jnp.right_shift(place_ref[0], 1), pair) for pair in pairs]

    def fetch(step, n):
        source = pl.ds(pl.multiple_of((first + step * GROUP) * HEAD_DIM, HEAD_DIM), wide)
        target = pl.ds(pl.multiple_of(step * wide, wide), wide)
        above = pl.ds(pl.multiple_of(spots[n] * rows, rows), rows)
        return pltpu.make_async_copy(
            q_source.at[above, source],
            q_ref.at[n * rows : (n + 1) * rows, target],
            sems.at[n, step],
        )

    def fetch_whole(step, m):
        source = pl.ds(pl.multiple_of((first + step * GROUP) * HEAD_DIM, HEAD_DIM), wide)
        target = pl.ds(pl.multiple_of(step * wide, wide), wide)
        return pltpu.make_async_copy(
            (k_source, v_source)[m].at[:, source],
            (k_ref, v_ref)[m].at[:, target],
            kv_sems.at[m, step],
        )

    for step in range(heads // GROUP):
        for m in range(2):
            fetch_whole(step, m).start()
        for n in range(len(pairs)):
            fetch(step, n).start()
    count = k_ref.shape[0]
    chunk = min(CHUNK, rows)
    chunks = rows // chunk
    chunk_bits = chunk.bit_length() - 1
    row_bits = rows.bit_length() - 1
    blocks = count // rows
    groups = chunk // SUB
    low_tile = first // PER_TILE
    tiles = (first + heads - 1) // PER_TILE + 1 - low_tile

    def span(n, c):
        return pl.ds(pl.multiple_of(spots[n] * rows + c * chunk, chunk), chunk)

    for tile in range(tiles):
        lanes = slice((low_tile + tile) * LANES, (low_tile + tile + 1) * LANES)
        for n in range(len(pairs)):
            for c in range(chunks):
                here = slice(n * rows + c * chunk, n * rows + (c + 1) * chunk)
                wt_ref[tile * LANES : (tile + 1) * LANES, here] = w_ref[span(n, c), lanes].T

    t = lax.broadcasted_iota(jnp.int32, (SUB, chunk), 1)
    s = lax.broadcasted_iota(jnp.int32, (SUB, chunk), 0)
    t_low, t_high = t & (SUB - 1), t >> SUB_BITS
    near_mix = jnp.where(s <= t_low, s ^ t_low, SUB)
    far_mix = []
    for a in range(max(1, groups // SUB)):
        s_high = s + SUB * a
        far_mix.append(jnp.where(t_high > s_high, t_high ^ s_high, 0))

    def group(step, carry):
        for m in range(2):
            fetch_whole(step, m).wait()
        for n in range(len(pairs)):
            fetch(step, n).wait()
        head = first + step * GROUP
        lane = pl.multiple_of(head // PER_TILE * LANES, LANES)
        base = head % PER_TILE * LEVELS
        rows_base = lane - low_tile * LANES + base
        shift = (LANES - base) % LANES
        weights = []
        for n in range(len(pairs)):
            above = pl.ds(pl.multiple_of(spots[n] * rows, rows), rows)
            weights.append(pltpu.roll(w_ref[above, pl.ds(lane, LANES)], shift, 1))
        sums, outer = {}, {}

        def columns(i):
            place = (step * GROUP + i) * HEAD_DIM
            return pl.ds(pl.multiple_of(place, HEAD_DIM), HEAD_DIM)

        def outer_tiers(i):
            held = columns(i)
            states = []
            for block in range(blocks - 1):
                here = slice(block * rows, (block + 1) * rows)
                states.append(dot(k_ref[here, held], v_ref[here, held], ((0,), (0,))))
            for n, spot in enumerate(spots):
                for bit in range(blocks.bit_length() - 1):
                    tier = jnp.zeros((HEAD_DIM, HEAD_DIM), jnp.float32)
                    for block, state in enumerate(states):
                        if not block >> bit & 1:
                            same = jnp.right_shift(spot, bit + 1) == block >> (bit + 1)
                            upper = (jnp.right_shift(spot, bit) & 1) == 1
                            tier += jnp.where(same & upper, state, jnp.float32(0.0))
                    outer[i, n, bit] = tier.astype(jnp.bfloat16)

        def scores_of(i, n, c):
            held = columns(i)
            here = slice(n * rows + c * chunk, n * rows + (c + 1) * chunk)
            q, k, v = q_ref[here, columns(i)], k_ref[span(n, c), held], v_ref[span(n, c), held]
            scores = dot(k, q, ((1,), (1,)))
            terms = []
            for bit in range(chunks.bit_length() - 1):
                if c >> bit & 1:
                    tier = sums[i, n, bit].astype(jnp.bfloat16)
                    terms.append((chunk_bits + 1 + bit, dot(q, tier)))
            for bit in range(blocks.bit_length() - 1):
                terms.append((row_bits + 1 + bit, dot(q, outer[i, n, bit])))
            if c + 1 < chunks:
                state = dot(k, v, ((0,), (0,)))
                for bit in range(chunks.bit_length() - 1):
                    if not c >> bit & 1:
                        fresh = c % (1 << bit) == 0
                        sums[i, n, bit] = state if fresh else sums[i, n, bit] + state
            return scores, terms

        def store(i, n, c, scores, terms):
            here = slice(n * rows + c * chunk, n * rows + (c + 1) * chunk)
            own_rows = pl.ds(pl.multiple_of(rows_base + i * LEVELS, LEVELS), LEVELS)
            near, far = factor_rows(wt_ref[own_rows, here], near_mix, far_mix)
            parts = []
            for r in range(groups):
                line = jnp.broadcast_to(far[r // SUB][r % SUB : r % SUB + 1], (SUB, chunk))
                factor = jnp.where(t_high == r, near, line)
                parts.append(scores[r * SUB : (r + 1) * SUB] * factor)
            weighted = jnp.concatenate(parts, axis=0).astype(jnp.bfloat16)
            total = dot(weighted, v_ref[span(n, c), columns(i)], ((0,), (0,)))
            for level, term in terms:
                column = i * LEVELS + level
                scale = weights[n][c * chunk : (c + 1) * chunk, column : column + 1]
                total += scale * term
            out_ref[here, columns(i)] = total

        waiting = []
        for i in range(GROUP):
            outer_tiers(i)
            for n in range(len(pairs)):
                for c in range(chunks):
                    waiting.append((i, n, c) + scores_of(i, n, c))
                    if len(waiting) > 2:
                        store(*waiting.pop(0))
        for unit in waiting:
            store(*unit)
        return carry

    lax.fori_loop(0, heads // GROUP, group, 0)


def inner_part(
    place, queries, keys, values, weights, chunk_first, start, heads, pairs, parts, after
):
    rows = 2 * queries.shape[0] // parts
    first = chunk_first + start
    tiles = (first + heads - 1) // PER_TILE + 1 - first // PER_TILE
    shape = (len(pairs) * rows, heads * HEAD_DIM)
    return pl.pallas_call(
        functools.partial(inner_kernel, first, heads, tuple(pairs), rows),
        in_specs=[pl.BlockSpec(memory_space=pltpu.SMEM), hbm(), hbm(), hbm(), local()]
        + [anywhere() for _ in after],
        out_specs=[local()] * 2,
        out_shape=[
            jax.ShapeDtypeStruct(shape, jnp.float32),
            jax.ShapeDtypeStruct(shape, queries.dtype),
        ],
        scratch_shapes=[
            pltpu.VMEM((queries.shape[0], shape[1]), keys.dtype),
            pltpu.VMEM((queries.shape[0], shape[1]), values.dtype),
            pltpu.VMEM((tiles * LANES, shape[0]), jnp.float32),
            pltpu.SemaphoreType.DMA((len(pairs), heads // GROUP)),
            pltpu.SemaphoreType.DMA((2, heads // GROUP)),
        ],
        compiler_params=params(12),
        cost_estimate=cost(pairs),
        name="inner_part",
    )(place, in_hbm(queries), in_hbm(keys), in_hbm(values), weights, *after)


def finish_kernel(
    first, start, heads, pairs, held, shift, levels, place_ref, q_ref, w_ref, inner_ref, *refs
):
    tiers = refs[:levels]
    outs = refs[len(refs) - 2 * len(pairs) :]
    local_bits = w_ref.shape[0].bit_length() - 1
    rows = outs[0].shape[0]
    flip = (place_ref[0] & 1) == 1

    def group(step, carry):
        head = first + step * GROUP
        lane = pl.multiple_of(head // PER_TILE * LANES, LANES)
        base = head % PER_TILE * LEVELS
        for n, pair in enumerate(pairs):
            spot = jnp.bitwise_xor(jnp.right_shift(place_ref[0], 1), pair)
            here = pl.ds(pl.multiple_of(spot * (2 * rows), 2 * rows), 2 * rows)
            weights = pltpu.roll(w_ref[here, pl.ds(lane, LANES)], (LANES - base) % LANES, 1)
            for i in range(GROUP):
                cols = pl.ds(pl.multiple_of((step * GROUP + i) * HEAD_DIM, HEAD_DIM), HEAD_DIM)
                spot_held = held.index(pair)
                own = slice(2 * spot_held * rows, 2 * (spot_held + 1) * rows)
                source = (shift + step * GROUP + i) * HEAD_DIM
                source = pl.ds(pl.multiple_of(source, HEAD_DIM), HEAD_DIM)
                q = q_ref[own, source]
                total = inner_ref[own, source]
                for m in range(levels):
                    level = i * LEVELS + local_bits + 1 + m
                    upper = place_ref[1 + m].astype(jnp.float32)
                    tier = tiers[m][start + step * GROUP + i]
                    total += (weights[:, level : level + 1] * upper) * dot(q, tier)
                top, bottom = total[:rows], total[rows:]
                outs[2 * n][:, cols] = jnp.where(flip, bottom, top).astype(jnp.bfloat16)
                outs[2 * n + 1][:, cols] = jnp.where(flip, top, bottom).astype(jnp.bfloat16)
        return carry

    lax.fori_loop(0, heads // GROUP, group, 0)


def finish(
    place, tiers, inner, weights, chunk_first, start, heads, pairs, parts, after
):
    total, queries, held, begin = inner
    rows = weights.shape[0] // parts
    outs = 2 * len(pairs)
    return pl.pallas_call(
        functools.partial(
            finish_kernel,
            chunk_first + start,
            start,
            heads,
            tuple(pairs),
            held,
            start - begin,
            len(tiers),
        ),
        in_specs=[pl.BlockSpec(memory_space=pltpu.SMEM)]
        + [local()] * (3 + len(tiers))
        + [anywhere() for _ in after],
        out_specs=[local()] * outs,
        out_shape=[
            jax.ShapeDtypeStruct((rows, heads * HEAD_DIM), jnp.bfloat16) for _ in range(outs)
        ],
        compiler_params=params(8),
        cost_estimate=cost(pairs),
        name="finish",
    )(place, queries, weights, total, *tiers, *after)


def gate_kernel(gain_ref, gate_ref, *refs):
    out_ref = refs[-1]
    tile = min(LANES * SUB, out_ref.shape[1])

    def columns(j, carry):
        here = pl.ds(pl.multiple_of(j * tile, tile), tile)
        half = gate_ref[:, here].astype(jnp.float32) * 0.5
        out_ref[:, here] = (half + half * jnp.tanh(half)) * gain_ref[:, here]
        return carry

    lax.fori_loop(0, out_ref.shape[1] // tile, columns, 0)


def gating(gain, gate, after):
    return pl.pallas_call(
        gate_kernel,
        in_specs=[local()] * 2 + [anywhere() for _ in after],
        out_specs=local(),
        out_shape=jax.ShapeDtypeStruct(gate.shape, jnp.float32),
        compiler_params=params(8),
        cost_estimate=TINY,
        name="gating",
    )(gain.reshape(1, gain.shape[0]), gate, *after)


def norm_kernel(layout, width, place_ref, gating_ref, *refs):
    out_ref = refs[-1]
    pieces = refs[:-1]
    tile = out_ref.shape[0]
    rows = pl.ds(pl.multiple_of(pl.program_id(0) * tile, tile), tile)
    square = None
    for ref in pieces:
        x = ref[rows, :].astype(jnp.float32)
        part = jnp.sum(x * x, axis=1, keepdims=True)
        square = part if square is None else square + part
    scale = lax.rsqrt(square / out_ref.shape[1] + 1e-06)
    for (step, start), ref in zip(layout, pieces):
        offset = pl.multiple_of(jnp.bitwise_xor(place_ref[0], step) * width + start, LANES)
        here = pl.ds(offset, ref.shape[1])
        x = ref[rows, :].astype(jnp.float32) * scale
        out_ref[:, here] = (x * gating_ref[rows, here]).astype(jnp.bfloat16)


def normalize(place, gated, layout, pieces, width):
    rows, features = gated.shape
    tile = min(64, rows)
    return pl.pallas_call(
        functools.partial(norm_kernel, layout, width),
        grid=(rows // tile,),
        in_specs=[pl.BlockSpec(memory_space=pltpu.SMEM)] + [local()] * (1 + len(pieces)),
        out_specs=pl.BlockSpec((tile, features), lambda i: (i, 0)),
        out_shape=jax.ShapeDtypeStruct((rows, features), jnp.bfloat16),
        compiler_params=params(8),
        cost_estimate=LONG,
        name="normalize",
    )(place, in_vmem(gated), *pieces)


def cut(heads):
    sizes = []
    for size in SIZES:
        if heads - sum(sizes) > size:
            sizes.append(size)
    return sizes + [heads - sum(sizes)]


def per_device(queries, key_vectors, value_vectors, level_weight, gate_values, norm_gain):
    count, width = queries.shape
    heads = width // HEAD_DIM
    blocks = lax.axis_size("seq")
    parts = lax.axis_size("head")
    seq_bits = blocks.bit_length() - 1
    block = lax.axis_index("seq")
    flags = [jnp.right_shift(block, m) & 1 for m in range(seq_bits)]
    place = jnp.stack([lax.axis_index("head")] + flags).astype(jnp.int32)

    sizes = cut(heads)
    chunks = range(len(sizes))
    firsts = [sum(sizes[:g]) for g in chunks]

    sends, tiers, inner = {}, {}, {}
    pieces, layout, arrived = [], [], {}
    last = {}

    def hop(g):
        m = len(tiers[g])
        pairs = [(i, i ^ 1 << m) for i in range(blocks)]
        tiers[g].append(lax.ppermute(sends[g], "seq", pairs))

    def state_step(g):
        sends[g] = block_states(
            key_vectors, value_vectors, firsts[g], sizes[g], tuple(last.values())
        )
        tiers[g] = []
        last["kernel"] = sends[g]
        hop(g)

    def add_step(g):
        if len(tiers[g]) < seq_bits:
            sends[g] = add_states(sends[g], tiers[g][-1], tuple(last.values()))
            last["kernel"] = sends[g]
            hop(g)

    def inner_step(g, pairs, start, size):
        total, held = inner_part(
            place,
            queries,
            key_vectors,
            value_vectors,
            level_weight,
            firsts[g],
            start,
            size,
            pairs,
            parts,
            tuple(last.values()),
        )
        inner[g] = total, held, tuple(pairs), start
        last["kernel"] = total

    def finish_step(g, pairs, start, size):
        behind = g - 2 if pairs[0] else g - 1 if g == len(sizes) - 1 else -1
        before = tuple(arrived.get(behind, ()))
        outs = finish(
            place,
            tiers[g],
            inner[g],
            level_weight,
            firsts[g],
            start,
            size,
            pairs,
            parts,
            tuple(last.values()) + before,
        )
        last["kernel"] = outs[-1]
        for step, out in enumerate(outs, 2 * pairs[0]):
            if step:
                out = lax.ppermute(out, "head", [(i, i ^ step) for i in range(parts)])
            pieces.append(out)
            layout.append((step, (firsts[g] + start) * HEAD_DIM))
            if pairs[0]:
                arrived.setdefault(g, []).append(out)

    far, near = list(range(1, parts // 2)), [0]
    for kind, g in ORDER:
        if g >= len(sizes):
            continue
        if kind == "S":
            state_step(g)
        if kind == "A":
            add_step(g)
        if kind == "I":
            inner_step(g, far, 0, sizes[g])
        if kind == "W":
            inner_step(g, far + near, 0, sizes[g])
        if kind == "F":
            for _ in range(seq_bits):
                add_step(g)
            finish_step(g, far, 0, sizes[g])
        if kind == "N":
            if 0 not in inner[g][2]:
                inner_step(g, near, 0, sizes[g])
            for start in range(0, sizes[g], SIZES[0]):
                size = min(SIZES[0], sizes[g] - start)
                finish_step(g, near, start, size)
    gated = gating(norm_gain, gate_values, tuple(last.values()))
    return normalize(place, gated, layout, pieces, width)


def solution(mesh):
    placed = (
        P("seq", "head"),
        P("seq", "head"),
        P("seq", "head"),
        P("seq", "head"),
        P(("seq", "head"), None),
        P(),
    )
    return jax.shard_map(
        per_device, mesh=mesh, in_specs=placed, out_specs=P(("seq", "head"), None), check_vma=False
    )
```

```python
import functools

import jax
import jax.numpy as jnp
from jax import lax
from jax.experimental import pallas as pl
from jax.experimental.pallas import tpu as pltpu
from jax.sharding import PartitionSpec as P

HEAD_DIM = 128
LEVELS = 16
CHUNK = 128
LANES = 128
SUB = 8
SUB_BITS = 3
GROUP = 2
PER_TILE = LANES // LEVELS
SIZES = (4, 4)
ORDER = (
    ("S", 0),
    ("S", 1),
    ("A", 0),
    ("S", 2),
    ("A", 0),
    ("A", 1),
    ("I", 0),
    ("F", 0),
    ("A", 1),
    ("A", 2),
    ("W", 1),
    ("A", 2),
    ("F", 1),
    ("I", 2),
    ("N", 1),
    ("F", 2),
    ("N", 0),
    ("N", 2),
)
TINY = pl.CostEstimate(flops=1024, bytes_accessed=1024, transcendentals=0)
LONG = pl.CostEstimate(flops=3 * 10**9, bytes_accessed=10**6, transcendentals=0)


def dot(a, b, dims=((1,), (0,))):
    return lax.dot_general(a, b, (dims, ((), ())), preferred_element_type=jnp.float32)


def anywhere():
    return pl.BlockSpec(memory_space=pl.ANY)


def cost(pairs):
    return LONG if pairs[0] else TINY


def local():
    return pl.BlockSpec(memory_space=pltpu.VMEM)


def params(mebibytes):
    return pltpu.CompilerParams(vmem_limit_bytes=mebibytes * 1024 * 1024)


def hbm():
    return pl.BlockSpec(memory_space=pltpu.HBM)


def in_hbm(array):
    return pltpu.with_memory_space_constraint(array, pltpu.HBM)


def in_vmem(array):
    return pltpu.with_memory_space_constraint(array, pltpu.VMEM)


def fetches(source_ref, held_ref, first, heads, sems):
    copies = []
    for n in range(heads // GROUP):
        source = pl.ds((first + n * GROUP) * HEAD_DIM, GROUP * HEAD_DIM)
        target = pl.ds(n * GROUP * HEAD_DIM, GROUP * HEAD_DIM)
        copies.append(
            pltpu.make_async_copy(source_ref.at[:, source], held_ref.at[:, target], sems.at[n])
        )
    return copies


def state_kernel(first, heads, k_ref, v_ref, *refs):
    rounded_ref, k_held, v_held, k_sems, v_sems = refs[-5:]
    k_copies = fetches(k_ref, k_held, first, heads, k_sems)
    v_copies = fetches(v_ref, v_held, first, heads, v_sems)
    for n in range(heads // GROUP):
        k_copies[n].start()
        v_copies[n].start()
    for n in range(heads // GROUP):
        k_copies[n].wait()
        v_copies[n].wait()
        for i in range(n * GROUP, (n + 1) * GROUP):
            here = slice(i * HEAD_DIM, (i + 1) * HEAD_DIM)
            state = dot(k_held[:, here], v_held[:, here], ((0,), (0,)))
            rounded_ref[i] = state.astype(jnp.bfloat16)


def block_states(keys, values, first, heads, after):
    held = pltpu.VMEM((keys.shape[0], heads * HEAD_DIM), keys.dtype)
    return pl.pallas_call(
        functools.partial(state_kernel, first, heads),
        in_specs=[hbm(), hbm()] + [anywhere() for _ in after],
        out_specs=local(),
        out_shape=jax.ShapeDtypeStruct((heads, HEAD_DIM, HEAD_DIM), jnp.bfloat16),
        scratch_shapes=[held, held] + [pltpu.SemaphoreType.DMA((heads // GROUP,))] * 2,
        compiler_params=params(12),
        cost_estimate=LONG,
        name="block_states",
    )(in_hbm(keys), in_hbm(values), *after)


def add_kernel(total_ref, held_ref, *refs):
    sum_ref = refs[-1]
    total = total_ref[...].astype(jnp.float32) + held_ref[...].astype(jnp.float32)
    sum_ref[...] = total.astype(jnp.bfloat16)


def add_states(total, held, after):
    return pl.pallas_call(
        add_kernel,
        in_specs=[local()] * 2 + [anywhere() for _ in after],
        out_specs=local(),
        out_shape=jax.ShapeDtypeStruct(total.shape, jnp.bfloat16),
        compiler_params=params(4),
        cost_estimate=LONG,
        name="add_states",
    )(in_vmem(total), held, *after)


def factor_rows(weights, near_mix, far_mix):
    chunk = weights.shape[1]
    bits = chunk.bit_length() - 1
    row = [jnp.broadcast_to(weights[l : l + 1], (SUB, chunk)) for l in range(bits + 1)]
    near = row[0]
    for level in range(1, SUB_BITS + 1):
        near = jnp.where(near_mix >= 1 << (level - 1), row[level], near)
    near = jnp.where(near_mix >= SUB, jnp.float32(0.0), near)
    far = []
    for mix in far_mix:
        value = jnp.zeros((SUB, chunk), jnp.float32)
        for level in range(SUB_BITS + 1, bits + 1):
            value = jnp.where(mix >= 1 << (level - SUB_BITS - 1), row[level], value)
        far.append(value)
    return near, far


def inner_kernel(
    first, heads, pairs, rows, place_ref, q_source, k_source, v_source, w_ref, *refs
):
    out_ref, q_ref, k_ref, v_ref, wt_ref, sems, kv_sems = refs[-7:]
    wide = GROUP * HEAD_DIM
    spots = [jnp.bitwise_xor(jnp.right_shift(place_ref[0], 1), pair) for pair in pairs]

    def fetch(step, n):
        source = pl.ds(pl.multiple_of((first + step * GROUP) * HEAD_DIM, HEAD_DIM), wide)
        target = pl.ds(pl.multiple_of(step * wide, wide), wide)
        above = pl.ds(pl.multiple_of(spots[n] * rows, rows), rows)
        return pltpu.make_async_copy(
            q_source.at[above, source],
            q_ref.at[n * rows : (n + 1) * rows, target],
            sems.at[n, step],
        )

    def fetch_whole(step, m):
        source = pl.ds(pl.multiple_of((first + step * GROUP) * HEAD_DIM, HEAD_DIM), wide)
        target = pl.ds(pl.multiple_of(step * wide, wide), wide)
        return pltpu.make_async_copy(
            (k_source, v_source)[m].at[:, source],
            (k_ref, v_ref)[m].at[:, target],
            kv_sems.at[m, step],
        )

    for step in range(heads // GROUP):
        for m in range(2):
            fetch_whole(step, m).start()
        for n in range(len(pairs)):
            fetch(step, n).start()
    count = k_ref.shape[0]
    chunk = min(CHUNK, rows)
    chunks = rows // chunk
    chunk_bits = chunk.bit_length() - 1
    row_bits = rows.bit_length() - 1
    blocks = count // rows
    groups = chunk // SUB
    low_tile = first // PER_TILE
    tiles = (first + heads - 1) // PER_TILE + 1 - low_tile

    def span(n, c):
        return pl.ds(pl.multiple_of(spots[n] * rows + c * chunk, chunk), chunk)

    for tile in range(tiles):
        lanes = slice((low_tile + tile) * LANES, (low_tile + tile + 1) * LANES)
        for n in range(len(pairs)):
            for c in range(chunks):
                here = slice(n * rows + c * chunk, n * rows + (c + 1) * chunk)
                wt_ref[tile * LANES : (tile + 1) * LANES, here] = w_ref[span(n, c), lanes].T

    t = lax.broadcasted_iota(jnp.int32, (SUB, chunk), 1)
    s = lax.broadcasted_iota(jnp.int32, (SUB, chunk), 0)
    t_low, t_high = t & (SUB - 1), t >> SUB_BITS
    near_mix = jnp.where(s <= t_low, s ^ t_low, SUB)
    far_mix = []
    for a in range(max(1, groups // SUB)):
        s_high = s + SUB * a
        far_mix.append(jnp.where(t_high > s_high, t_high ^ s_high, 0))

    def group(step, carry):
        for m in range(2):
            fetch_whole(step, m).wait()
        for n in range(len(pairs)):
            fetch(step, n).wait()
        head = first + step * GROUP
        lane = pl.multiple_of(head // PER_TILE * LANES, LANES)
        base = head % PER_TILE * LEVELS
        rows_base = lane - low_tile * LANES + base
        shift = (LANES - base) % LANES
        weights = []
        for n in range(len(pairs)):
            above = pl.ds(pl.multiple_of(spots[n] * rows, rows), rows)
            weights.append(pltpu.roll(w_ref[above, pl.ds(lane, LANES)], shift, 1))
        sums, outer = {}, {}

        def columns(i):
            place = (step * GROUP + i) * HEAD_DIM
            return pl.ds(pl.multiple_of(place, HEAD_DIM), HEAD_DIM)

        def outer_tiers(i):
            held = columns(i)
            states = []
            for block in range(blocks - 1):
                here = slice(block * rows, (block + 1) * rows)
                states.append(dot(k_ref[here, held], v_ref[here, held], ((0,), (0,))))
            for n, spot in enumerate(spots):
                for bit in range(blocks.bit_length() - 1):
                    tier = jnp.zeros((HEAD_DIM, HEAD_DIM), jnp.float32)
                    for block, state in enumerate(states):
                        if not block >> bit & 1:
                            same = jnp.right_shift(spot, bit + 1) == block >> (bit + 1)
                            upper = (jnp.right_shift(spot, bit) & 1) == 1
                            tier += jnp.where(same & upper, state, jnp.float32(0.0))
                    outer[i, n, bit] = tier.astype(jnp.bfloat16)

        def scores_of(i, n, c):
            held = columns(i)
            here = slice(n * rows + c * chunk, n * rows + (c + 1) * chunk)
            q, k, v = q_ref[here, columns(i)], k_ref[span(n, c), held], v_ref[span(n, c), held]
            scores = dot(k, q, ((1,), (1,)))
            terms = []
            for bit in range(chunks.bit_length() - 1):
                if c >> bit & 1:
                    tier = sums[i, n, bit].astype(jnp.bfloat16)
                    terms.append((chunk_bits + 1 + bit, dot(q, tier)))
            for bit in range(blocks.bit_length() - 1):
                terms.append((row_bits + 1 + bit, dot(q, outer[i, n, bit])))
            if c + 1 < chunks:
                state = dot(k, v, ((0,), (0,)))
                for bit in range(chunks.bit_length() - 1):
                    if not c >> bit & 1:
                        fresh = c % (1 << bit) == 0
                        sums[i, n, bit] = state if fresh else sums[i, n, bit] + state
            return scores, terms

        def store(i, n, c, scores, terms):
            here = slice(n * rows + c * chunk, n * rows + (c + 1) * chunk)
            own_rows = pl.ds(pl.multiple_of(rows_base + i * LEVELS, LEVELS), LEVELS)
            near, far = factor_rows(wt_ref[own_rows, here], near_mix, far_mix)
            parts = []
            for r in range(groups):
                line = jnp.broadcast_to(far[r // SUB][r % SUB : r % SUB + 1], (SUB, chunk))
                factor = jnp.where(t_high == r, near, line)
                parts.append(scores[r * SUB : (r + 1) * SUB] * factor)
            weighted = jnp.concatenate(parts, axis=0).astype(jnp.bfloat16)
            total = dot(weighted, v_ref[span(n, c), columns(i)], ((0,), (0,)))
            for level, term in terms:
                column = i * LEVELS + level
                scale = weights[n][c * chunk : (c + 1) * chunk, column : column + 1]
                total += scale * term
            out_ref[here, columns(i)] = total

        waiting = []
        for i in range(GROUP):
            outer_tiers(i)
            for n in range(len(pairs)):
                for c in range(chunks):
                    waiting.append((i, n, c) + scores_of(i, n, c))
                    if len(waiting) > 2:
                        store(*waiting.pop(0))
        for unit in waiting:
            store(*unit)
        return carry

    lax.fori_loop(0, heads // GROUP, group, 0)


def inner_part(
    place, queries, keys, values, weights, chunk_first, start, heads, pairs, parts, after
):
    rows = 2 * queries.shape[0] // parts
    first = chunk_first + start
    tiles = (first + heads - 1) // PER_TILE + 1 - first // PER_TILE
    shape = (len(pairs) * rows, heads * HEAD_DIM)
    return pl.pallas_call(
        functools.partial(inner_kernel, first, heads, tuple(pairs), rows),
        in_specs=[pl.BlockSpec(memory_space=pltpu.SMEM), hbm(), hbm(), hbm(), local()]
        + [anywhere() for _ in after],
        out_specs=[local()] * 2,
        out_shape=[
            jax.ShapeDtypeStruct(shape, jnp.float32),
            jax.ShapeDtypeStruct(shape, queries.dtype),
        ],
        scratch_shapes=[
            pltpu.VMEM((queries.shape[0], shape[1]), keys.dtype),
            pltpu.VMEM((queries.shape[0], shape[1]), values.dtype),
            pltpu.VMEM((tiles * LANES, shape[0]), jnp.float32),
            pltpu.SemaphoreType.DMA((len(pairs), heads // GROUP)),
            pltpu.SemaphoreType.DMA((2, heads // GROUP)),
        ],
        compiler_params=params(12),
        cost_estimate=cost(pairs),
        name="inner_part",
    )(place, in_hbm(queries), in_hbm(keys), in_hbm(values), weights, *after)


def finish_kernel(
    first, start, heads, pairs, held, shift, levels, place_ref, q_ref, w_ref, inner_ref, *refs
):
    tiers = refs[:levels]
    outs = refs[len(refs) - 2 * len(pairs) :]
    local_bits = w_ref.shape[0].bit_length() - 1
    rows = outs[0].shape[0]
    flip = (place_ref[0] & 1) == 1

    def group(step, carry):
        head = first + step * GROUP
        lane = pl.multiple_of(head // PER_TILE * LANES, LANES)
        base = head % PER_TILE * LEVELS
        for n, pair in enumerate(pairs):
            spot = jnp.bitwise_xor(jnp.right_shift(place_ref[0], 1), pair)
            here = pl.ds(pl.multiple_of(spot * (2 * rows), 2 * rows), 2 * rows)
            weights = pltpu.roll(w_ref[here, pl.ds(lane, LANES)], (LANES - base) % LANES, 1)
            for i in range(GROUP):
                cols = pl.ds(pl.multiple_of((step * GROUP + i) * HEAD_DIM, HEAD_DIM), HEAD_DIM)
                spot_held = held.index(pair)
                own = slice(2 * spot_held * rows, 2 * (spot_held + 1) * rows)
                source = (shift + step * GROUP + i) * HEAD_DIM
                source = pl.ds(pl.multiple_of(source, HEAD_DIM), HEAD_DIM)
                q = q_ref[own, source]
                total = inner_ref[own, source]
                for m in range(levels):
                    level = i * LEVELS + local_bits + 1 + m
                    upper = place_ref[1 + m].astype(jnp.float32)
                    tier = tiers[m][start + step * GROUP + i]
                    total += (weights[:, level : level + 1] * upper) * dot(q, tier)
                top, bottom = total[:rows], total[rows:]
                outs[2 * n][:, cols] = jnp.where(flip, bottom, top).astype(jnp.bfloat16)
                outs[2 * n + 1][:, cols] = jnp.where(flip, top, bottom).astype(jnp.bfloat16)
        return carry

    lax.fori_loop(0, heads // GROUP, group, 0)


def finish(
    place, tiers, inner, weights, chunk_first, start, heads, pairs, parts, after
):
    total, queries, held, begin = inner
    rows = weights.shape[0] // parts
    outs = 2 * len(pairs)
    return pl.pallas_call(
        functools.partial(
            finish_kernel,
            chunk_first + start,
            start,
            heads,
            tuple(pairs),
            held,
            start - begin,
            len(tiers),
        ),
        in_specs=[pl.BlockSpec(memory_space=pltpu.SMEM)]
        + [local()] * (3 + len(tiers))
        + [anywhere() for _ in after],
        out_specs=[local()] * outs,
        out_shape=[
            jax.ShapeDtypeStruct((rows, heads * HEAD_DIM), jnp.bfloat16) for _ in range(outs)
        ],
        compiler_params=params(8),
        cost_estimate=cost(pairs),
        name="finish",
    )(place, queries, weights, total, *tiers, *after)


def gate_kernel(gain_ref, gate_ref, *refs):
    out_ref = refs[-1]
    tile = min(LANES * SUB, out_ref.shape[1])

    def columns(j, carry):
        here = pl.ds(pl.multiple_of(j * tile, tile), tile)
        half = gate_ref[:, here].astype(jnp.float32) * 0.5
        out_ref[:, here] = (half + half * jnp.tanh(half)) * gain_ref[:, here]
        return carry

    lax.fori_loop(0, out_ref.shape[1] // tile, columns, 0)


def gating(gain, gate, after):
    return pl.pallas_call(
        gate_kernel,
        in_specs=[local()] * 2 + [anywhere() for _ in after],
        out_specs=local(),
        out_shape=jax.ShapeDtypeStruct(gate.shape, jnp.float32),
        compiler_params=params(8),
        cost_estimate=TINY,
        name="gating",
    )(gain.reshape(1, gain.shape[0]), gate, *after)


def norm_kernel(layout, width, place_ref, gating_ref, *refs):
    out_ref = refs[-1]
    pieces = refs[:-1]
    tile = out_ref.shape[0]
    rows = pl.ds(pl.multiple_of(pl.program_id(0) * tile, tile), tile)
    square = None
    for ref in pieces:
        x = ref[rows, :].astype(jnp.float32)
        part = jnp.sum(x * x, axis=1, keepdims=True)
        square = part if square is None else square + part
    scale = lax.rsqrt(square / out_ref.shape[1] + 1e-06)
    for (step, start), ref in zip(layout, pieces):
        offset = pl.multiple_of(jnp.bitwise_xor(place_ref[0], step) * width + start, LANES)
        here = pl.ds(offset, ref.shape[1])
        x = ref[rows, :].astype(jnp.float32) * scale
        out_ref[:, here] = (x * gating_ref[rows, here]).astype(jnp.bfloat16)


def normalize(place, gated, layout, pieces, width):
    rows, features = gated.shape
    tile = min(64, rows)
    return pl.pallas_call(
        functools.partial(norm_kernel, layout, width),
        grid=(rows // tile,),
        in_specs=[pl.BlockSpec(memory_space=pltpu.SMEM)] + [local()] * (1 + len(pieces)),
        out_specs=pl.BlockSpec((tile, features), lambda i: (i, 0)),
        out_shape=jax.ShapeDtypeStruct((rows, features), jnp.bfloat16),
        compiler_params=params(8),
        cost_estimate=LONG,
        name="normalize",
    )(place, in_vmem(gated), *pieces)


def cut(heads):
    sizes = []
    for size in SIZES:
        if heads - sum(sizes) > size:
            sizes.append(size)
    return sizes + [heads - sum(sizes)]


def per_device(queries, key_vectors, value_vectors, level_weight, gate_values, norm_gain):
    count, width = queries.shape
    heads = width // HEAD_DIM
    blocks = lax.axis_size("seq")
    parts = lax.axis_size("head")
    seq_bits = blocks.bit_length() - 1
    block = lax.axis_index("seq")
    flags = [jnp.right_shift(block, m) & 1 for m in range(seq_bits)]
    place = jnp.stack([lax.axis_index("head")] + flags).astype(jnp.int32)

    sizes = cut(heads)
    chunks = range(len(sizes))
    firsts = [sum(sizes[:g]) for g in chunks]

    sends, tiers, inner = {}, {}, {}
    pieces, layout, arrived = [], [], {}
    last = {}

    def hop(g):
        m = len(tiers[g])
        pairs = [(i, i ^ 1 << m) for i in range(blocks)]
        tiers[g].append(lax.ppermute(sends[g], "seq", pairs))

    def state_step(g):
        sends[g] = block_states(
            key_vectors, value_vectors, firsts[g], sizes[g], tuple(last.values())
        )
        tiers[g] = []
        last["kernel"] = sends[g]
        hop(g)

    def add_step(g):
        if len(tiers[g]) < seq_bits:
            sends[g] = add_states(sends[g], tiers[g][-1], tuple(last.values()))
            last["kernel"] = sends[g]
            hop(g)

    def inner_step(g, pairs, start, size):
        total, held = inner_part(
            place,
            queries,
            key_vectors,
            value_vectors,
            level_weight,
            firsts[g],
            start,
            size,
            pairs,
            parts,
            tuple(last.values()),
        )
        inner[g] = total, held, tuple(pairs), start
        last["kernel"] = total

    def finish_step(g, pairs, start, size):
        behind = g - 2 if pairs[0] else g - 1 if g == len(sizes) - 1 else -1
        before = tuple(arrived.get(behind, ()))
        outs = finish(
            place,
            tiers[g],
            inner[g],
            level_weight,
            firsts[g],
            start,
            size,
            pairs,
            parts,
            tuple(last.values()) + before,
        )
        last["kernel"] = outs[-1]
        for step, out in enumerate(outs, 2 * pairs[0]):
            if step:
                out = lax.ppermute(out, "head", [(i, i ^ step) for i in range(parts)])
            pieces.append(out)
            layout.append((step, (firsts[g] + start) * HEAD_DIM))
            if pairs[0]:
                arrived.setdefault(g, []).append(out)

    far, near = list(range(1, parts // 2)), [0]
    for kind, g in ORDER:
        if g >= len(sizes):
            continue
        if kind == "S":
            state_step(g)
        if kind == "A":
            add_step(g)
        if kind == "I":
            inner_step(g, far, 0, sizes[g])
        if kind == "W":
            inner_step(g, far + near, 0, sizes[g])
        if kind == "F":
            for _ in range(seq_bits):
                add_step(g)
            finish_step(g, far, 0, sizes[g])
        if kind == "N":
            if 0 not in inner[g][2]:
                inner_step(g, near, 0, sizes[g])
            for start in range(0, sizes[g], SIZES[0]):
                size = min(SIZES[0], sizes[g] - start)
                finish_step(g, near, start, size)
    gated = gating(norm_gain, gate_values, tuple(last.values()))
    return normalize(place, gated, layout, pieces, width)


def solution(mesh):
    placed = (
        P("seq", "head"),
        P("seq", "head"),
        P("seq", "head"),
        P("seq", "head"),
        P(("seq", "head"), None),
        P(),
    )
    return jax.shard_map(
        per_device, mesh=mesh, in_specs=placed, out_specs=P(("seq", "head"), None), check_vma=False
    )
```
